32 devices in a mesh: groups: 2 (over y), wide: 4 (over z), tp: 2 (over x), sub: 2 (over core).
Axes of the slice: x: 2, y: 2, z: 4, core: 2. Of those that a mesh axis runs over, the one named last changes fastest.
Arguments:
- hidden: bfloat16 [2, 4096, 8192], P(None, ('groups', 'wide'), ('tp', 'sub')), parts along dimension 1, may hold values from -40 to 40
- target_subgroup: int32 [4096, 1], P(('groups', 'wide')), parts along dimension 0, may hold values from 0 to 3; in each aligned block of 512 rows (0 to 511, 512 to 1023, ...) at most 256 rows name the same one
- token_position: int32 [4096], P(('groups', 'wide')), parts along dimension 0, may hold values from 0 to 4095
- adapter_of_row: int32 [4096], P(('groups', 'wide')), parts along dimension 0, may hold values from 0 to 7
- request_length: int32 [4096], P(('groups', 'wide')), parts along dimension 0, may hold values from 1 to 4096
- input_norm_scale: bfloat16 [2, 8192], P(None, ('tp', 'sub')), may hold values from 0.099609375 to 1.8984375
- key_value_weight: bfloat16 [2, 8192, 2048], P(None, ('tp', 'sub')), may hold values from -0.0625 to 0.0625
- adapter_down_weight: bfloat16 [2, 8192, 128], P(None, ('tp', 'sub')), may hold values from -0.0625 to 0.0625
- adapter_up_weight: bfloat16 [2, 128, 2048], P(None, None, ('tp', 'sub')), may hold values from -0.75 to 0.75
Outputs:
- kv_cache: bfloat16 [2, 8192, 2048], P(None, ('groups', 'wide'), ('tp', 'sub')), parts along dimension 1
The draws below stay inside these ranges and needn't reach their ends.
There are 2 independent parts, one for each index of `groups`. The reference program is written for one: setup_inputs(seed, part) draws one part's arguments, and reference() takes and returns one part's arrays. A program takes and returns all parts, laid end to end along the dimension named above; an argument that names none is the same for every part. Nothing has to cross between parts.
Inputs may be any that keep to these rules, and one draw needn't show every extreme that they name: `target_subgroup`: in the rows of one holder no serving subgroup is named by more than 256 rows, a bound that some block reaches.
All inputs are finite; a program needn't handle non-finite values.
Results may differ from the reference program's by a relative error of at most 0.0054.
Values may be sent and summed in bfloat16 or wider, within the bound.
A program may use at most 192 MiB of HBM per device.

```python
import math
import jax
import jax.numpy as jnp
import numpy as np
from jax import lax

MODEL_WIDTH = 8192
KEY_VALUE_HEADS = 8
HEAD_SIZE = 128
ADAPTER_COUNT = 8
ADAPTER_RANK = 16
LAYER_COUNT = 2
CTX = 4096
SLOTS = 512
CAP = 256
ROWS = 2048
N_WIDE = 4


def draw_hidden(key, part):
    key = jax.random.fold_in(key, 11)
    key_base, key_row, key_col = jax.random.split(key, 3)
    row_scale = jnp.exp(jax.random.uniform(key_row, (LAYER_COUNT, ROWS, 1), jnp.float32, -0.6931, 0.6931))
    ramp = 3.0 ** (jnp.arange(MODEL_WIDTH, dtype=jnp.float32) / MODEL_WIDTH)
    col_scale = jnp.exp(jax.random.uniform(key_col, (1, 1, MODEL_WIDTH), jnp.float32, -0.5, 0.5)) * ramp[None, None, :]
    values = jnp.clip(jax.random.normal(key_base, (LAYER_COUNT, ROWS, MODEL_WIDTH), jnp.float32), -4.0, 4.0)
    return (values * row_scale * col_scale).astype(jnp.bfloat16)


def place_ends(array, own_key, smallest, top_value):
    index_at = [jax.random.randint(jax.random.fold_in(own_key, axis), (), 0, length) for axis, length in enumerate(array.shape)]
    longest = array.shape.index(max(array.shape))
    beside = index_at[:longest] + [(index_at[longest] + 1) % array.shape[longest]] + index_at[longest + 1:]
    return array.at[tuple(index_at)].set(smallest).at[tuple(beside)].set(top_value)


def levels(stream_key, dims, shards, low, top_value):
    loudness = 1.0
    for axis_at, blocks in shards:
        draws = jax.random.uniform(jax.random.fold_in(jax.random.fold_in(stream_key, 6), axis_at), (blocks,), jnp.float32, low / len(shards), top_value / len(shards))
        loudness = loudness * jnp.repeat(jnp.exp(draws), dims[axis_at] // blocks).reshape((-1,) + (1,) * (len(dims) - 1 - axis_at))
    return loudness


def routed_block(stream_key, own, number, rows, count, top, bound, skew):
    ranking = jax.random.permutation(stream_key, count)
    packed, usual = shares(count, rows * top, bound, skew, True), shares(count, rows * top, bound, skew, False)
    places = jnp.arange(count)

    def named(lengths, offset_by):
        used = int((lengths > 0).sum())
        fixed = max(1, used // 4)
        shifted = fixed + (places - fixed + offset_by * (used - fixed)) % max(1, count - fixed)
        return jnp.zeros((count,), jnp.int32).at[ranking[jnp.where(places < fixed, places, shifted)]].set(jnp.asarray(lengths, jnp.int32))

    lengths = jnp.where(number % 4 == 0, named(packed, number // 4), named(usual, number - number // 4 - 1))
    mixed = jax.random.permutation(jax.random.fold_in(own, 3), count)
    source_of, receiver = mixed[0:count // 2 * 2:2], mixed[1:count // 2 * 2:2]
    room = jnp.minimum(lengths[source_of] - 1, bound - lengths[receiver]) // 2
    room = jnp.where((source_of == ranking[0]) | (receiver == ranking[0]) | (lengths[receiver] == 0), 0, jnp.maximum(room, 0))
    shifted = jax.random.randint(jax.random.fold_in(own, 4), (count // 2,), 0, 1 << 20) % (room + 1)
    lengths = lengths.at[source_of].add(-shifted).at[receiver].add(shifted)
    items = jnp.searchsorted(jnp.cumsum(lengths), jnp.arange(rows * top), side="right").astype(jnp.int32)
    table = items.reshape(top, rows).T
    table = table[jax.random.permutation(jax.random.fold_in(own, 1), rows)]
    offset_by = jax.random.randint(jax.random.fold_in(own, 2), (rows, 1), 0, top)
    return jnp.take_along_axis(table, (jnp.arange(top)[None, :] + offset_by) % top, axis=1)


def shares(count, total, most, slope, full):
    loads = [(1 << 20) // math.isqrt(rank ** slope) + 1 for rank in range(1, count + 1)]
    largest = most if full else min(most, max(-(-total // count), total * loads[0] // sum(loads)))
    least = 1 if total - largest >= count - 1 else 0
    holding, surplus = [largest] + [least] * (count - 1), total - largest - least * (count - 1)
    while surplus > 0:
        free = [i for i in range(1, count) if holding[i] < largest] or [i for i in range(1, count) if holding[i] < most]
        mass, left = sum([loads[i] for i in free]), surplus
        for i in free:
            more = min(most - holding[i], max(1, left * loads[i] // mass), surplus)
            holding[i] = holding[i] + more
            surplus = surplus - more
    return np.array(holding)


def centred(rng, shape, spread, limit, pieces=(), held_as=jnp.bfloat16):
    level = levels(rng, shape, pieces, -0.22, 0.18) if pieces else 1.0
    array = jax.random.normal(rng, shape, jnp.float32) * spread * level
    return jnp.minimum(jnp.maximum(array, -limit), limit).astype(held_as)


def setup_inputs(seed: int = 0, part: int = 0) -> dict:
    arg_keys = jax.random.split(jax.random.key(seed), 10)
    own_keys = jax.random.split(jax.random.fold_in(arg_keys[9], part), 10)
    hidden = draw_hidden(jax.random.fold_in(jax.random.fold_in(arg_keys[9], part), 71), part)
    target_subgroup_keys = jax.random.split(jax.random.fold_in(own_keys[1], 1), ROWS // SLOTS)
    target_subgroup_turns = jax.random.permutation(jax.random.fold_in(own_keys[1], 3), ROWS // SLOTS)
    target_subgroup = jax.vmap(lambda own, number: routed_block(jax.random.fold_in(own_keys[1], 2), own, number, SLOTS, N_WIDE, 1, CAP, 2))(target_subgroup_keys, target_subgroup_turns).reshape((ROWS, 1))
    token_position = place_ends(jax.random.randint(own_keys[2], (ROWS,), 0, CTX), jax.random.fold_in(own_keys[2], 1), 0, CTX - 1).astype(jnp.int32)
    adapter_of_row = place_ends(jax.random.randint(own_keys[3], (ROWS,), 0, ADAPTER_COUNT), jax.random.fold_in(own_keys[3], 1), 0, ADAPTER_COUNT - 1).astype(jnp.int32)
    request_length = place_ends(jax.random.randint(own_keys[4], (ROWS,), 1, CTX + 1), jax.random.fold_in(own_keys[4], 1), 1, CTX).astype(jnp.int32)
    input_norm_scale = jnp.clip(1.0 + 0.18 * jax.random.normal(arg_keys[5], (LAYER_COUNT, MODEL_WIDTH), jnp.float32), 0.099609375, 1.8984375).astype(jnp.bfloat16)
    key_value_weight = centred(arg_keys[6], (LAYER_COUNT, MODEL_WIDTH, 2 * KEY_VALUE_HEADS * HEAD_SIZE), MODEL_WIDTH ** -0.5, 0.0625, ((1, 4),))
    adapter_down_weight = centred(arg_keys[7], (LAYER_COUNT, MODEL_WIDTH, ADAPTER_COUNT * ADAPTER_RANK), MODEL_WIDTH ** -0.5, 0.0625, ((1, 4),))
    adapter_up_weight = centred(arg_keys[8], (LAYER_COUNT, ADAPTER_COUNT * ADAPTER_RANK, 2 * KEY_VALUE_HEADS * HEAD_SIZE), (4 * ADAPTER_RANK) ** -0.5, 0.75, ((2, 4),))
    return dict(hidden=hidden, target_subgroup=target_subgroup, token_position=token_position, adapter_of_row=adapter_of_row, request_length=request_length, input_norm_scale=input_norm_scale, key_value_weight=key_value_weight, adapter_down_weight=adapter_down_weight, adapter_up_weight=adapter_up_weight)


EPS = 1e-05
ROPE_BASE = 500000.0
ADAPTER_SCALE = 2.0

def rotate(fresh, position):
    count = fresh.shape[0]
    heads = fresh.shape[1] // (2 * HEAD_SIZE)
    blocks = fresh.reshape(count, heads, 2, HEAD_SIZE)
    half = HEAD_SIZE // 2
    freq = ROPE_BASE ** (-(jnp.arange(half, dtype=jnp.float32) * 2.0 / HEAD_SIZE))
    angle = position.astype(jnp.float32)[:, None] * freq[None, :]
    cosine = jnp.cos(angle)[:, None, :]
    sine = jnp.sin(angle)[:, None, :]
    keys = blocks[:, :, 0]
    first = keys[..., :half]
    second = keys[..., half:]
    turned = jnp.concatenate([first * cosine - second * sine, second * cosine + first * sine], -1)
    return jnp.stack([turned, blocks[:, :, 1]], 2).reshape(count, heads * 2 * HEAD_SIZE)

def rebuild_layer_cache(rows_h, gain, weight, down_map, up_map, position, adapter, valid_mask):
    wide_rows = rows_h.astype(jnp.float32)
    total_ss = lax.optimization_barrier(jnp.sum(wide_rows * wide_rows, 1))
    adapter_scaling = lax.rsqrt(total_ss / MODEL_WIDTH + EPS)
    scaled = (wide_rows * gain.astype(jnp.float32)[None, :]).astype(jnp.bfloat16)
    base = jnp.dot(scaled, weight, preferred_element_type=jnp.float32)
    down_projected = jnp.dot(scaled, down_map, preferred_element_type=jnp.float32)
    owner = jnp.arange(ADAPTER_COUNT * ADAPTER_RANK, dtype=jnp.int32) // ADAPTER_RANK
    picked_adapter = adapter[:, None] == owner[None, :]
    low_rank_rows = jnp.where(picked_adapter, ADAPTER_SCALE * adapter_scaling[:, None] * down_projected, 0.0).astype(jnp.bfloat16)
    fresh = adapter_scaling[:, None] * base + jnp.dot(low_rank_rows, up_map, preferred_element_type=jnp.float32)
    rotated = rotate(fresh, position)
    return jnp.where(valid_mask[:, None], rotated, 0.0).astype(jnp.bfloat16)

def reference(hidden, target_subgroup, token_position, adapter_of_row, request_length, input_norm_scale, key_value_weight, adapter_down_weight, adapter_up_weight):
    valid_mask = token_position < request_length
    layer_list = [rebuild_layer_cache(hidden[layer_number], input_norm_scale[layer_number], key_value_weight[layer_number], adapter_down_weight[layer_number], adapter_up_weight[layer_number], token_position, adapter_of_row, valid_mask) for layer_number in range(LAYER_COUNT)]
    restored = jnp.stack(layer_list)
    target = target_subgroup[:, 0].reshape(N_WIDE, SLOTS)
    onehot = (target[:, :, None] == jnp.arange(N_WIDE, dtype=jnp.int32)[None, None, :]).astype(jnp.int32)
    rank = lax.optimization_barrier(jnp.sum(jnp.cumsum(onehot, 1) * onehot, 2)) - 1
    holder = jnp.arange(N_WIDE, dtype=jnp.int32)[:, None]
    slot_index = (target * (N_WIDE * CAP) + holder * CAP + rank).reshape(-1).astype(jnp.int32)
    cache = jnp.zeros((LAYER_COUNT, N_WIDE * N_WIDE * CAP, restored.shape[2]), jnp.bfloat16)
    return cache.at[:, slot_index].set(restored)
```

```python
import functools

import jax
import jax.numpy as jnp
from jax import lax
from jax.experimental import pallas as pl
from jax.experimental.pallas import tpu as pltpu
from jax.sharding import PartitionSpec as P

MODEL_WIDTH = 8192
HEAD_SIZE = 128
ADAPTER_COUNT = 8
ADAPTER_RANK = 16
EPS = 1e-05
ROPE_BASE = 500000.0
ADAPTER_SCALE = 2.0
UNIT = HEAD_SIZE
STAT_ROWS = 24
F32, BF16 = jnp.float32, jnp.bfloat16


def restore_kernel(
    sizes,
    hidden_hbm,
    weight_hbm,
    down_hbm,
    up_ref,
    gain_ref,
    target_ref,
    position_ref,
    adapter_ref,
    length_ref,
    freq_ref,
    out_hbm,
    hidden_buf,
    scaled,
    weight_buf,
    down_buf,
    own_acc,
    core_out,
    core_in,
    x_out,
    x_in,
    stat_out,
    stat_in,
    low_rows,
    scale_rows,
    cos_tab,
    sin_tab,
    pick,
    z_out,
    hidden_sem,
    weight_sem,
    down_sem,
    core_send,
    core_recv,
    x_send,
    x_recv,
    stat_send,
    stat_recv,
    z_send,
    z_recv,
    z_local,
):
    layers, slots, features, block, tp_size, sub_size, width = sizes
    capacity = 2 * slots // width
    units = block // UNIT
    chunks = layers * units
    peers = tp_size * sub_size
    half_cols = tp_size * UNIT

    tp = lax.axis_index("tp")
    sub = lax.axis_index("sub")
    wide = lax.axis_index("wide")

    def peer_id(d):
        dt, ds = d // sub_size, d % sub_size
        return {"tp": lax.rem(tp + dt, tp_size), "sub": lax.rem(sub + ds, sub_size)}

    def wide_id(dw):
        return {"wide": lax.rem(wide + dw, width)}

    def hidden_copy(layer):
        return pltpu.make_async_copy(hidden_hbm.at[layer], hidden_buf.at[layer], hidden_sem.at[layer])

    def down_copy(layer):
        return pltpu.make_async_copy(down_hbm.at[layer], down_buf.at[layer], down_sem.at[layer])

    def weight_copies(chunk):
        layer, unit = chunk // units, chunk % units
        copies = []
        for ds in range(sub_size):
            for dt in range(tp_size):
                t = lax.rem(tp + dt, tp_size)
                s = lax.rem(sub + ds, sub_size)
                column = pl.multiple_of((t * sub_size + s) * block + unit * UNIT, UNIT)
                place = ds * tp_size + dt
                copies.append(
                    pltpu.make_async_copy(
                        weight_hbm.at[layer, :, pl.ds(column, UNIT)],
                        weight_buf.at[chunk, :, pl.ds(place * UNIT, UNIT)],
                        weight_sem.at[chunk, place],
                    )
                )
        return copies

    def core_copy(chunk):
        return pltpu.make_async_remote_copy(
            src_ref=core_out.at[chunk],
            dst_ref=core_in.at[chunk],
            send_sem=core_send.at[chunk],
            recv_sem=core_recv.at[chunk],
            device_id={"sub": lax.rem(sub + 1, sub_size)},
            device_id_type=pl.DeviceIdType.MESH,
        )

    def x_copy(chunk, dt):
        return pltpu.make_async_remote_copy(
            src_ref=x_out.at[chunk, dt - 1],
            dst_ref=x_in.at[chunk, dt - 1],
            send_sem=x_send.at[chunk, dt - 1],
            recv_sem=x_recv.at[chunk, dt - 1],
            device_id={"tp": lax.rem(tp + dt, tp_size)},
            device_id_type=pl.DeviceIdType.MESH,
        )

    def stat_copy(layer, d):
        return pltpu.make_async_remote_copy(
            src_ref=stat_out.at[layer],
            dst_ref=stat_in.at[layer, d - 1],
            send_sem=stat_send.at[layer, d - 1],
            recv_sem=stat_recv.at[layer, d - 1],
            device_id=peer_id(d),
            device_id_type=pl.DeviceIdType.MESH,
        )

    def z_copy(chunk, dw, holder):
        layer, unit = chunk // units, chunk % units
        goal = lax.rem(wide + dw, width)
        return pltpu.make_async_remote_copy(
            src_ref=z_out.at[chunk, pl.ds(pl.multiple_of(goal * capacity, 16), capacity), :],
            dst_ref=out_hbm.at[
                layer,
                pl.ds(pl.multiple_of(holder * capacity, 16), capacity),
                pl.ds(pl.multiple_of(unit * UNIT, UNIT), UNIT),
            ],
            send_sem=z_send.at[chunk, dw - 1],
            recv_sem=z_recv.at[chunk, dw - 1],
            device_id=wide_id(dw),
            device_id_type=pl.DeviceIdType.MESH,
        )

    def z_own(chunk):
        layer, unit = chunk // units, chunk % units
        rows = pl.ds(pl.multiple_of(wide * capacity, 16), capacity)
        return pltpu.make_async_copy(
            z_out.at[chunk, rows, :],
            out_hbm.at[layer, rows, pl.ds(pl.multiple_of(unit * UNIT, UNIT), UNIT)],
            z_local.at[chunk],
        )

    def scale_hidden(layer):
        hidden_copy(layer).wait()
        step_rows = 128

        @pl.loop(0, slots // step_rows)
        def _(r):
            rows = pl.ds(pl.multiple_of(r * step_rows, step_rows), step_rows)
            squares = jnp.zeros((step_rows, 128), F32)
            for k in range(features // 128):
                columns = pl.ds(k * 128, 128)
                values = hidden_buf[layer, rows, columns].astype(F32)
                gain = gain_ref[layer, columns].astype(F32)
                squares += values * values
                scaled[layer, rows, columns] = (values * gain[None, :]).astype(BF16)
            total = jnp.sum(squares.T, axis=0, keepdims=True)
            stat_out[layer, pl.ds(ADAPTER_RANK, 8), rows] = jnp.broadcast_to(total, (8, step_rows))

    def send_stats(layer):
        down_copy(layer).wait()
        down = jnp.dot(scaled[layer], down_buf[layer], preferred_element_type=F32).T
        adapter = adapter_ref[...]
        picked = jnp.zeros((ADAPTER_RANK, slots), F32)
        for a in range(ADAPTER_COUNT):
            picked += jnp.where(adapter == a, down[a * ADAPTER_RANK : (a + 1) * ADAPTER_RANK], 0.0)
        stat_out[layer, pl.ds(0, ADAPTER_RANK), :] = picked
        for d in range(1, peers):
            stat_copy(layer, d).start()

    def take_stats(layer):
        total = stat_out[layer]
        for d in range(1, peers):
            stat_copy(layer, d).wait_recv()
            total += stat_in[layer, d - 1]
        scale = lax.rsqrt(total[ADAPTER_RANK : ADAPTER_RANK + 1] / MODEL_WIDTH + EPS)
        low = ADAPTER_SCALE * scale * total[:ADAPTER_RANK]
        adapter = adapter_ref[...]
        spread = jnp.concatenate(
            [jnp.where(adapter == a, low, 0.0) for a in range(ADAPTER_COUNT)], axis=0
        )
        low_rows[layer] = spread.T.astype(BF16)
        scale_rows[layer] = jnp.broadcast_to(scale, (UNIT, slots)).T

    def make_tables():
        position = position_ref[...]
        angle = freq_ref[...] * position.astype(F32)
        cosine, sine = jnp.cos(angle), jnp.sin(angle)
        cos_tab[0] = jnp.concatenate([cosine, cosine], axis=0).T
        sin_tab[0] = jnp.concatenate([-sine, sine], axis=0).T
        cos_tab[1] = jnp.ones((slots, UNIT), F32)
        sin_tab[1] = jnp.zeros((slots, UNIT), F32)
        target = target_ref[...]
        lanes = max(width, 16)
        onehot = lax.broadcasted_iota(jnp.int32, (lanes, slots), 0) == target
        before = lax.broadcasted_iota(jnp.int32, (slots, slots), 0) <= lax.broadcasted_iota(
            jnp.int32, (slots, slots), 1
        )
        counted = jnp.dot(
            jnp.where(onehot, 1.0, 0.0).astype(BF16),
            jnp.where(before, 1.0, 0.0).astype(BF16),
            preferred_element_type=F32,
        )
        rank = jnp.sum(jnp.where(onehot, counted, 0.0), axis=0, keepdims=True).astype(jnp.int32) - 1
        place = target * capacity + rank
        place = jnp.where(position < length_ref[...], place, -1)

        @pl.loop(0, width * capacity // 128)
        def _(r):
            index = lax.broadcasted_iota(jnp.int32, (128, slots), 0) + r * 128
            pick[pl.ds(pl.multiple_of(r * 128, 128), 128), :] = jnp.where(
                index == place, 1.0, 0.0
            ).astype(BF16)

    def project(chunk):
        for copy in weight_copies(chunk):
            copy.wait()
        layer = chunk // units
        core_out[chunk] = jnp.dot(
            scaled[layer], weight_buf[chunk, :, half_cols:], preferred_element_type=F32
        ).astype(BF16)
        core_copy(chunk).start()
        own_acc[chunk] = jnp.dot(
            scaled[layer], weight_buf[chunk, :, :half_cols], preferred_element_type=F32
        )

    def pass_on(chunk):
        core_copy(chunk).wait_recv()
        for dt in range(1, tp_size):
            columns = pl.ds(dt * UNIT, UNIT)
            x_out[chunk, dt - 1] = (
                own_acc[chunk, :, columns] + core_in[chunk, :, columns].astype(F32)
            ).astype(BF16)
            x_copy(chunk, dt).start()

    def finish(chunk):
        layer, unit = chunk // units, chunk % units
        base = own_acc[chunk, :, pl.ds(0, UNIT)] + core_in[chunk, :, pl.ds(0, UNIT)].astype(F32)
        for dt in range(1, tp_size):
            x_copy(chunk, dt).wait_recv()
            base += x_in[chunk, dt - 1].astype(F32)
        fresh = scale_rows[layer] * base + jnp.dot(
            low_rows[layer], up_ref[layer, unit], preferred_element_type=F32
        )
        kind = unit % 2
        rotated = (
            fresh * cos_tab[kind] + pltpu.roll(fresh, HEAD_SIZE // 2, 1) * sin_tab[kind]
        ).astype(BF16)
        z_out[chunk] = jnp.dot(pick[...], rotated, preferred_element_type=F32).astype(BF16)
        for dw in range(width - 1, 0, -1):
            z_copy(chunk, dw, wide).start()
        z_own(chunk).start()

    hidden_copy(0).start()
    for copy in weight_copies(0):
        copy.start()
    down_copy(0).start()

    barrier = pltpu.get_barrier_semaphore()
    for d in range(1, peers):
        pl.semaphore_signal(barrier, inc=1, device_id=peer_id(d), device_id_type=pl.DeviceIdType.MESH)
    for dw in range(1, width):
        pl.semaphore_signal(barrier, inc=1, device_id=wide_id(dw), device_id_type=pl.DeviceIdType.MESH)

    @pl.loop(1, chunks)
    def _(chunk):
        for copy in weight_copies(chunk):
            copy.start()

    for layer in range(1, layers):
        hidden_copy(layer).start()
        down_copy(layer).start()
    scale_hidden(0)
    pl.semaphore_wait(barrier, peers - 1 + width - 1)

    @pl.loop(0, chunks + 2)
    def _(step):
        @pl.when(step < chunks)
        def _():
            project(step)

        @pl.when(step == 0)
        def _():
            send_stats(0)
            pass_on(0)
            make_tables()

        @pl.when(step == 1)
        def _():
            take_stats(0)
            for layer in range(1, layers):
                scale_hidden(layer)
                send_stats(layer)

        @pl.when((step >= 2) & (step <= chunks))
        def _():
            pass_on(step - 1)

        @pl.when(step >= 2)
        def _():
            finish(step - 2)

        @pl.when(step == 2)
        def _():
            for layer in range(1, layers):
                take_stats(layer)

    for layer in range(layers):
        for d in range(1, peers):
            stat_copy(layer, d).wait_send()

    @pl.loop(0, chunks)
    def _(chunk):
        core_copy(chunk).wait_send()
        for dt in range(1, tp_size):
            x_copy(chunk, dt).wait_send()
        for dw in range(1, width):
            z_copy(chunk, dw, wide).wait_send()
            z_copy(chunk, dw, lax.rem(wide - dw + width, width)).wait_recv()
        z_own(chunk).wait()


def shards(
    sizes_of_mesh,
    hidden,
    target_subgroup,
    token_position,
    adapter_of_row,
    request_length,
    input_norm_scale,
    key_value_weight,
    adapter_down_weight,
    adapter_up_weight,
):
    tp_size, sub_size, width = sizes_of_mesh
    layers, slots, features = hidden.shape
    block = adapter_up_weight.shape[2]
    units = block // UNIT
    chunks = layers * units
    peers = tp_size * sub_size
    capacity = 2 * slots // width
    half = HEAD_SIZE // 2
    freq = ROPE_BASE ** (-(jnp.arange(half, dtype=F32) * 2.0 / HEAD_SIZE))
    up_units = adapter_up_weight.reshape(layers, -1, units, UNIT).transpose(0, 2, 1, 3)
    sizes = (layers, slots, features, block, tp_size, sub_size, width)
    hbm = pl.BlockSpec(memory_space=pl.ANY)
    vmem = pl.BlockSpec(memory_space=pltpu.VMEM)
    dma = pltpu.SemaphoreType.DMA
    columns = key_value_weight.shape[2]
    ranks = adapter_down_weight.shape[2]
    return pl.pallas_call(
        functools.partial(restore_kernel, sizes),
        out_shape=jax.ShapeDtypeStruct((layers, width * capacity, block), BF16),
        in_specs=[hbm, hbm, hbm] + [vmem] * 7,
        out_specs=hbm,
        scratch_shapes=[
            pltpu.VMEM((layers, slots, features), BF16),
            pltpu.VMEM((layers, slots, features), BF16),
            pltpu.VMEM((chunks, features, peers * UNIT), BF16),
            pltpu.VMEM((layers, features, ranks), BF16),
            pltpu.VMEM((chunks, slots, tp_size * UNIT), F32),
            pltpu.VMEM((chunks, slots, tp_size * UNIT), BF16),
            pltpu.VMEM((chunks, slots, tp_size * UNIT), BF16),
            pltpu.VMEM((chunks, tp_size - 1, slots, UNIT), BF16),
            pltpu.VMEM((chunks, tp_size - 1, slots, UNIT), BF16),
            pltpu.VMEM((layers, STAT_ROWS, slots), F32),
            pltpu.VMEM((layers, peers - 1, STAT_ROWS, slots), F32),
            pltpu.VMEM((layers, slots, ranks), BF16),
            pltpu.VMEM((layers, slots, UNIT), F32),
            pltpu.VMEM((2, slots, UNIT), F32),
            pltpu.VMEM((2, slots, UNIT), F32),
            pltpu.VMEM((width * capacity, slots), BF16),
            pltpu.VMEM((chunks, width * capacity, UNIT), BF16),
            dma((layers,)),
            dma((chunks, peers)),
            dma((layers,)),
            dma((chunks,)),
            dma((chunks,)),
            dma((chunks, tp_size - 1)),
            dma((chunks, tp_size - 1)),
            dma((layers, peers - 1)),
            dma((layers, peers - 1)),
            dma((chunks, width - 1)),
            dma((chunks, width - 1)),
            dma((chunks,)),
        ],
        compiler_params=pltpu.CompilerParams(
            collective_id=0, has_side_effects=True, vmem_limit_bytes=56 * 1024 * 1024
        ),
        cost_estimate=pl.CostEstimate(
            flops=2 * layers * slots * features * columns,
            bytes_accessed=2 * layers * features * columns,
            transcendentals=0,
        ),
        name="restore_rows",
    )(
        hidden,
        key_value_weight,
        adapter_down_weight,
        up_units,
        input_norm_scale,
        target_subgroup.reshape(1, slots),
        token_position.reshape(1, slots),
        adapter_of_row.reshape(1, slots),
        request_length.reshape(1, slots),
        freq.reshape(half, 1),
    )


def solution(mesh):
    sizes_of_mesh = (mesh.shape["tp"], mesh.shape["sub"], mesh.shape["wide"])
    return jax.shard_map(
        functools.partial(shards, sizes_of_mesh),
        mesh=mesh,
        in_specs=(
            P(None, ("groups", "wide"), ("tp", "sub")),
            P(("groups", "wide"), None),
            P(("groups", "wide")),
            P(("groups", "wide")),
            P(("groups", "wide")),
            P(None, ("tp", "sub")),
            P(None, ("tp", "sub"), None),
            P(None, ("tp", "sub"), None),
            P(None, None, ("tp", "sub")),
        ),
        out_specs=P(None, ("groups", "wide"), ("tp", "sub")),
        check_vma=False,
    )
```

```python
import functools

import jax
import jax.numpy as jnp
import numpy as np
from jax import lax
from jax.experimental import pallas as pl
from jax.experimental.pallas import tpu as pltpu
from jax.sharding import PartitionSpec as P

MODEL_WIDTH = 8192
HEAD_SIZE = 128
ADAPTER_COUNT = 8
ADAPTER_RANK = 16
EPS = 1e-05
ROPE_BASE = 500000.0
ADAPTER_SCALE = 2.0
UNIT = HEAD_SIZE
STAT_ROWS = 24
F32, BF16 = jnp.float32, jnp.bfloat16


def restore_kernel(
    sizes,
    hidden_hbm,
    weight_hbm,
    down_hbm,
    up_ref,
    gain_ref,
    target_ref,
    position_ref,
    adapter_ref,
    length_ref,
    freq_ref,
    out_hbm,
    hidden_buf,
    scaled,
    weight_buf,
    down_buf,
    own_acc,
    core_out,
    core_in,
    x_out,
    x_in,
    stat_out,
    stat_in,
    low_rows,
    scale_rows,
    cos_tab,
    sin_tab,
    pick,
    z_out,
    hidden_sem,
    weight_sem,
    down_sem,
    core_send,
    core_recv,
    x_send,
    x_recv,
    stat_send,
    stat_recv,
    z_send,
    z_recv,
    z_local,
):
    layers, slots, features, block, tp_size, sub_size, width = sizes
    capacity = 2 * slots // width
    units = block // UNIT
    chunks = layers * units
    peers = tp_size * sub_size
    half_cols = tp_size * UNIT

    tp = lax.axis_index("tp")
    sub = lax.axis_index("sub")
    wide = lax.axis_index("wide")

    def peer_id(d):
        dt, ds = d // sub_size, d % sub_size
        return {"tp": lax.rem(tp + dt, tp_size), "sub": lax.rem(sub + ds, sub_size)}

    def wide_id(dw):
        return {"wide": lax.rem(wide + dw, width)}

    def hidden_copy(layer):
        return pltpu.make_async_copy(hidden_hbm.at[layer], hidden_buf.at[layer], hidden_sem.at[layer])

    def down_copy(layer):
        return pltpu.make_async_copy(down_hbm.at[layer], down_buf.at[layer], down_sem.at[layer])

    def weight_copies(chunk):
        layer, unit = chunk // units, chunk % units
        copies = []
        for ds in range(sub_size):
            for dt in range(tp_size):
                t = lax.rem(tp + dt, tp_size)
                s = lax.rem(sub + ds, sub_size)
                column = pl.multiple_of((t * sub_size + s) * block + unit * UNIT, UNIT)
                place = ds * tp_size + dt
                copies.append(
                    pltpu.make_async_copy(
                        weight_hbm.at[layer, :, pl.ds(column, UNIT)],
                        weight_buf.at[chunk, :, pl.ds(place * UNIT, UNIT)],
                        weight_sem.at[chunk, place],
                    )
                )
        return copies

    def core_copy(chunk):
        return pltpu.make_async_remote_copy(
            src_ref=core_out.at[chunk],
            dst_ref=core_in.at[chunk],
            send_sem=core_send.at[chunk],
            recv_sem=core_recv.at[chunk],
            device_id={"sub": lax.rem(sub + 1, sub_size)},
            device_id_type=pl.DeviceIdType.MESH,
        )

    def x_copy(chunk, dt):
        return pltpu.make_async_remote_copy(
            src_ref=x_out.at[chunk, dt - 1],
            dst_ref=x_in.at[chunk, dt - 1],
            send_sem=x_send.at[chunk, dt - 1],
            recv_sem=x_recv.at[chunk, dt - 1],
            device_id={"tp": lax.rem(tp + dt, tp_size)},
            device_id_type=pl.DeviceIdType.MESH,
        )

    def stat_copy(layer, d):
        return pltpu.make_async_remote_copy(
            src_ref=stat_out.at[layer],
            dst_ref=stat_in.at[layer, d - 1],
            send_sem=stat_send.at[layer, d - 1],
            recv_sem=stat_recv.at[layer, d - 1],
            device_id=peer_id(d),
            device_id_type=pl.DeviceIdType.MESH,
        )

    def z_copy(chunk, dw, holder):
        layer, unit = chunk // units, chunk % units
        goal = lax.rem(wide + dw, width)
        return pltpu.make_async_remote_copy(
            src_ref=z_out.at[chunk, pl.ds(pl.multiple_of(goal * capacity, 16), capacity), :],
            dst_ref=out_hbm.at[
                layer,
                pl.ds(pl.multiple_of(holder * capacity, 16), capacity),
                pl.ds(pl.multiple_of(unit * UNIT, UNIT), UNIT),
            ],
            send_sem=z_send.at[chunk, dw - 1],
            recv_sem=z_recv.at[chunk, dw - 1],
            device_id=wide_id(dw),
            device_id_type=pl.DeviceIdType.MESH,
        )

    def z_own(chunk):
        layer, unit = chunk // units, chunk % units
        rows = pl.ds(pl.multiple_of(wide * capacity, 16), capacity)
        return pltpu.make_async_copy(
            z_out.at[chunk, rows, :],
            out_hbm.at[layer, rows, pl.ds(pl.multiple_of(unit * UNIT, UNIT), UNIT)],
            z_local.at[chunk],
        )

    def scale_hidden(layer):
        hidden_copy(layer).wait()
        step_rows = 128

        @pl.loop(0, slots // step_rows)
        def _(r):
            rows = pl.ds(pl.multiple_of(r * step_rows, step_rows), step_rows)
            squares = jnp.zeros((step_rows, 128), F32)
            for k in range(features // 128):
                columns = pl.ds(k * 128, 128)
                values = hidden_buf[layer, rows, columns].astype(F32)
                gain = gain_ref[layer, columns].astype(F32)
                squares += values * values
                scaled[layer, rows, columns] = (values * gain[None, :]).astype(BF16)
            total = jnp.sum(squares.T, axis=0, keepdims=True)
            stat_out[layer, pl.ds(ADAPTER_RANK, 8), rows] = jnp.broadcast_to(total, (8, step_rows))

    def send_stats(layer):
        down_copy(layer).wait()
        down = jnp.dot(scaled[layer], down_buf[layer], preferred_element_type=F32).T
        adapter = adapter_ref[...]
        picked = jnp.zeros((ADAPTER_RANK, slots), F32)
        for a in range(ADAPTER_COUNT):
            picked += jnp.where(adapter == a, down[a * ADAPTER_RANK : (a + 1) * ADAPTER_RANK], 0.0)
        stat_out[layer, pl.ds(0, ADAPTER_RANK), :] = picked
        for d in range(1, peers):
            stat_copy(layer, d).start()

    def take_stats(layer):
        total = stat_out[layer]
        for d in range(1, peers):
            stat_copy(layer, d).wait_recv()
            total += stat_in[layer, d - 1]
        scale = lax.rsqrt(total[ADAPTER_RANK : ADAPTER_RANK + 1] / MODEL_WIDTH + EPS)
        low = ADAPTER_SCALE * scale * total[:ADAPTER_RANK]
        adapter = adapter_ref[...]
        spread = jnp.concatenate(
            [jnp.where(adapter == a, low, 0.0) for a in range(ADAPTER_COUNT)], axis=0
        )
        low_rows[layer] = spread.T.astype(BF16)
        scale_rows[layer] = jnp.broadcast_to(scale, (UNIT, slots)).T

    def make_tables():
        position = position_ref[...]
        angle = freq_ref[...] * position.astype(F32)
        cosine, sine = jnp.cos(angle), jnp.sin(angle)
        cos_tab[0] = jnp.concatenate([cosine, cosine], axis=0).T
        sin_tab[0] = jnp.concatenate([-sine, sine], axis=0).T
        cos_tab[1] = jnp.ones((slots, UNIT), F32)
        sin_tab[1] = jnp.zeros((slots, UNIT), F32)
        target = target_ref[...]
        lanes = max(width, 16)
        onehot = lax.broadcasted_iota(jnp.int32, (lanes, slots), 0) == target
        before = lax.broadcasted_iota(jnp.int32, (slots, slots), 0) <= lax.broadcasted_iota(
            jnp.int32, (slots, slots), 1
        )
        counted = jnp.dot(
            jnp.where(onehot, 1.0, 0.0).astype(BF16),
            jnp.where(before, 1.0, 0.0).astype(BF16),
            preferred_element_type=F32,
        )
        rank = jnp.sum(jnp.where(onehot, counted, 0.0), axis=0, keepdims=True).astype(jnp.int32) - 1
        place = target * capacity + rank
        place = jnp.where(position < length_ref[...], place, -1)

        @pl.loop(0, width * capacity // 128)
        def _(r):
            index = lax.broadcasted_iota(jnp.int32, (128, slots), 0) + r * 128
            pick[pl.ds(pl.multiple_of(r * 128, 128), 128), :] = jnp.where(
                index == place, 1.0, 0.0
            ).astype(BF16)

    def project(chunk):
        for copy in weight_copies(chunk):
            copy.wait()
        layer = chunk // units
        core_out[chunk] = jnp.dot(
            scaled[layer], weight_buf[chunk, :, half_cols:], preferred_element_type=F32
        ).astype(BF16)
        core_copy(chunk).start()
        own_acc[chunk] = jnp.dot(
            scaled[layer], weight_buf[chunk, :, :half_cols], preferred_element_type=F32
        )

    def pass_on(chunk):
        core_copy(chunk).wait_recv()
        for dt in range(1, tp_size):
            columns = pl.ds(dt * UNIT, UNIT)
            x_out[chunk, dt - 1] = (
                own_acc[chunk, :, columns] + core_in[chunk, :, columns].astype(F32)
            ).astype(BF16)
            x_copy(chunk, dt).start()

    def finish(chunk):
        layer, unit = chunk // units, chunk % units
        base = own_acc[chunk, :, pl.ds(0, UNIT)] + core_in[chunk, :, pl.ds(0, UNIT)].astype(F32)
        for dt in range(1, tp_size):
            x_copy(chunk, dt).wait_recv()
            base += x_in[chunk, dt - 1].astype(F32)
        fresh = scale_rows[layer] * base + jnp.dot(
            low_rows[layer],
            up_ref[layer, :, pl.ds(pl.multiple_of(unit * UNIT, UNIT), UNIT)],
            preferred_element_type=F32,
        )
        kind = unit % 2
        rotated = (
            fresh * cos_tab[kind] + pltpu.roll(fresh, HEAD_SIZE // 2, 1) * sin_tab[kind]
        ).astype(BF16)
        z_out[chunk] = jnp.dot(pick[...], rotated, preferred_element_type=F32).astype(BF16)
        for dw in range(width - 1, 0, -1):
            z_copy(chunk, dw, wide).start()
        z_own(chunk).start()

    hidden_copy(0).start()
    for copy in weight_copies(0):
        copy.start()
    down_copy(0).start()

    barrier = pltpu.get_barrier_semaphore()
    for d in range(1, peers):
        pl.semaphore_signal(barrier, inc=1, device_id=peer_id(d), device_id_type=pl.DeviceIdType.MESH)
    for dw in range(1, width):
        pl.semaphore_signal(barrier, inc=1, device_id=wide_id(dw), device_id_type=pl.DeviceIdType.MESH)

    scale_hidden(0)

    @pl.loop(1, chunks)
    def _(chunk):
        for copy in weight_copies(chunk):
            copy.start()

    for layer in range(1, layers):
        hidden_copy(layer).start()
        down_copy(layer).start()
    pl.semaphore_wait(barrier, peers - 1 + width - 1)

    @pl.loop(0, chunks + 1)
    def _(step):
        @pl.when(step == 2)
        def _():
            for layer in range(1, layers):
                scale_hidden(layer)

        @pl.when(step < chunks)
        def _():
            project(step)

        @pl.when(step == 0)
        def _():
            send_stats(0)

        @pl.when(step == 1)
        def _():
            make_tables()
            take_stats(0)

        @pl.when(step == 2)
        def _():
            for layer in range(1, layers):
                send_stats(layer)

        @pl.when(step < chunks)
        def _():
            pass_on(step)

        @pl.when(step == 3)
        def _():
            for layer in range(1, layers):
                take_stats(layer)

        @pl.when(step >= 1)
        def _():
            finish(step - 1)

    for layer in range(layers):
        for d in range(1, peers):
            stat_copy(layer, d).wait_send()

    @pl.loop(0, chunks)
    def _(chunk):
        core_copy(chunk).wait_send()
        for dt in range(1, tp_size):
            x_copy(chunk, dt).wait_send()
        for dw in range(1, width):
            z_copy(chunk, dw, wide).wait_send()
            z_copy(chunk, dw, lax.rem(wide - dw + width, width)).wait_recv()
        z_own(chunk).wait()


def shards(
    sizes_of_mesh,
    hidden,
    target_subgroup,
    token_position,
    adapter_of_row,
    request_length,
    input_norm_scale,
    key_value_weight,
    adapter_down_weight,
    adapter_up_weight,
):
    tp_size, sub_size, width = sizes_of_mesh
    layers, slots, features = hidden.shape
    block = adapter_up_weight.shape[2]
    units = block // UNIT
    chunks = layers * units
    peers = tp_size * sub_size
    capacity = 2 * slots // width
    half = HEAD_SIZE // 2
    freq = (ROPE_BASE ** (-np.arange(half) * 2.0 / HEAD_SIZE)).astype(np.float32)
    sizes = (layers, slots, features, block, tp_size, sub_size, width)
    hbm = pl.BlockSpec(memory_space=pl.ANY)
    vmem = pl.BlockSpec(memory_space=pltpu.VMEM)
    dma = pltpu.SemaphoreType.DMA
    columns = key_value_weight.shape[2]
    ranks = adapter_down_weight.shape[2]
    return pl.pallas_call(
        functools.partial(restore_kernel, sizes),
        out_shape=jax.ShapeDtypeStruct((layers, width * capacity, block), BF16),
        in_specs=[hbm, hbm, hbm] + [vmem] * 7,
        out_specs=hbm,
        scratch_shapes=[
            pltpu.VMEM((layers, slots, features), BF16),
            pltpu.VMEM((layers, slots, features), BF16),
            pltpu.VMEM((chunks, features, peers * UNIT), BF16),
            pltpu.VMEM((layers, features, ranks), BF16),
            pltpu.VMEM((chunks, slots, tp_size * UNIT), F32),
            pltpu.VMEM((chunks, slots, tp_size * UNIT), BF16),
            pltpu.VMEM((chunks, slots, tp_size * UNIT), BF16),
            pltpu.VMEM((chunks, tp_size - 1, slots, UNIT), BF16),
            pltpu.VMEM((chunks, tp_size - 1, slots, UNIT), BF16),
            pltpu.VMEM((layers, STAT_ROWS, slots), F32),
            pltpu.VMEM((layers, peers - 1, STAT_ROWS, slots), F32),
            pltpu.VMEM((layers, slots, ranks), BF16),
            pltpu.VMEM((layers, slots, UNIT), F32),
            pltpu.VMEM((2, slots, UNIT), F32),
            pltpu.VMEM((2, slots, UNIT), F32),
            pltpu.VMEM((width * capacity, slots), BF16),
            pltpu.VMEM((chunks, width * capacity, UNIT), BF16),
            dma((layers,)),
            dma((chunks, peers)),
            dma((layers,)),
            dma((chunks,)),
            dma((chunks,)),
            dma((chunks, tp_size - 1)),
            dma((chunks, tp_size - 1)),
            dma((layers, peers - 1)),
            dma((layers, peers - 1)),
            dma((chunks, width - 1)),
            dma((chunks, width - 1)),
            dma((chunks,)),
        ],
        compiler_params=pltpu.CompilerParams(
            collective_id=0, has_side_effects=True, vmem_limit_bytes=56 * 1024 * 1024
        ),
        cost_estimate=pl.CostEstimate(
            flops=2 * layers * slots * features * columns,
            bytes_accessed=2 * layers * features * columns,
            transcendentals=0,
        ),
        name="restore_rows",
    )(
        hidden,
        key_value_weight,
        adapter_down_weight,
        adapter_up_weight,
        input_norm_scale,
        target_subgroup.reshape(1, slots),
        token_position.reshape(1, slots),
        adapter_of_row.reshape(1, slots),
        request_length.reshape(1, slots),
        jnp.asarray(freq.reshape(half, 1)),
    )


def solution(mesh):
    sizes_of_mesh = (mesh.shape["tp"], mesh.shape["sub"], mesh.shape["wide"])
    return jax.shard_map(
        functools.partial(shards, sizes_of_mesh),
        mesh=mesh,
        in_specs=(
            P(None, ("groups", "wide"), ("tp", "sub")),
            P(("groups", "wide"), None),
            P(("groups", "wide")),
            P(("groups", "wide")),
            P(("groups", "wide")),
            P(None, ("tp", "sub")),
            P(None, ("tp", "sub"), None),
            P(None, ("tp", "sub"), None),
            P(None, None, ("tp", "sub")),
        ),
        out_specs=P(None, ("groups", "wide"), ("tp", "sub")),
        check_vma=False,
    )
```

```python
import functools

import jax
import jax.numpy as jnp
import numpy as np
from jax import lax
from jax.experimental import pallas as pl
from jax.experimental.pallas import tpu as pltpu
from jax.sharding import PartitionSpec as P

MODEL_WIDTH = 8192
HEAD_SIZE = 128
ADAPTER_COUNT = 8
ADAPTER_RANK = 16
EPS = 1e-05
ROPE_BASE = 500000.0
ADAPTER_SCALE = 2.0
UNIT = HEAD_SIZE
STAT_ROWS = 24
F32, BF16 = jnp.float32, jnp.bfloat16


def restore_kernel(
    sizes,
    hidden_hbm,
    weight_hbm,
    down_hbm,
    up_ref,
    gain_ref,
    target_ref,
    position_ref,
    adapter_ref,
    length_ref,
    freq_ref,
    held,
    hidden_buf,
    scaled,
    weight_buf,
    down_buf,
    own_acc,
    core_out,
    core_in,
    x_out,
    x_in,
    stat_out,
    stat_in,
    low_rows,
    scale_rows,
    cos_tab,
    sin_tab,
    pick,
    z_out,
    hidden_sem,
    weight_sem,
    down_sem,
    core_send,
    core_recv,
    x_send,
    x_recv,
    stat_send,
    stat_recv,
    z_send,
    z_recv,
    z_local,
):
    layers, slots, features, block, tp_size, sub_size, width = sizes
    capacity = 2 * slots // width
    units = block // UNIT
    chunks = layers * units
    peers = tp_size * sub_size
    half_cols = tp_size * UNIT

    tp = lax.axis_index("tp")
    sub = lax.axis_index("sub")
    wide = lax.axis_index("wide")

    def peer_id(d):
        dt, ds = d // sub_size, d % sub_size
        return {"tp": lax.rem(tp + dt, tp_size), "sub": lax.rem(sub + ds, sub_size)}

    def wide_id(dw):
        return {"wide": lax.rem(wide + dw, width)}

    def hidden_copy(layer):
        return pltpu.make_async_copy(hidden_hbm.at[layer], hidden_buf.at[layer], hidden_sem.at[layer])

    def down_copy(layer):
        return pltpu.make_async_copy(down_hbm.at[layer], down_buf.at[layer], down_sem.at[layer])

    def weight_copies(chunk):
        layer, unit = chunk // units, chunk % units
        copies = []
        for ds in range(sub_size):
            for dt in range(tp_size):
                t = lax.rem(tp + dt, tp_size)
                s = lax.rem(sub + ds, sub_size)
                column = pl.multiple_of((t * sub_size + s) * block + unit * UNIT, UNIT)
                place = ds * tp_size + dt
                copies.append(
                    pltpu.make_async_copy(
                        weight_hbm.at[layer, :, pl.ds(column, UNIT)],
                        weight_buf.at[chunk, :, pl.ds(place * UNIT, UNIT)],
                        weight_sem.at[chunk, place],
                    )
                )
        return copies

    def core_copy(chunk):
        return pltpu.make_async_remote_copy(
            src_ref=core_out.at[chunk],
            dst_ref=core_in.at[chunk],
            send_sem=core_send.at[chunk],
            recv_sem=core_recv.at[chunk],
            device_id={"sub": lax.rem(sub + 1, sub_size)},
            device_id_type=pl.DeviceIdType.MESH,
        )

    def x_copy(chunk, dt):
        return pltpu.make_async_remote_copy(
            src_ref=x_out.at[chunk, dt - 1],
            dst_ref=x_in.at[chunk, dt - 1],
            send_sem=x_send.at[chunk, dt - 1],
            recv_sem=x_recv.at[chunk, dt - 1],
            device_id={"tp": lax.rem(tp + dt, tp_size)},
            device_id_type=pl.DeviceIdType.MESH,
        )

    def stat_copy(layer, d):
        return pltpu.make_async_remote_copy(
            src_ref=stat_out.at[layer],
            dst_ref=stat_in.at[layer, d - 1],
            send_sem=stat_send.at[layer, d - 1],
            recv_sem=stat_recv.at[layer, d - 1],
            device_id=peer_id(d),
            device_id_type=pl.DeviceIdType.MESH,
        )

    def z_copy(chunk, dw, holder):
        goal = lax.rem(wide + dw, width)
        return pltpu.make_async_remote_copy(
            src_ref=z_out.at[chunk, pl.ds(pl.multiple_of(goal * capacity, 16), capacity), :],
            dst_ref=held.at[chunk, pl.ds(pl.multiple_of(holder * capacity, 16), capacity), :],
            send_sem=z_send.at[chunk, dw - 1],
            recv_sem=z_recv.at[chunk, dw - 1],
            device_id=wide_id(dw),
            device_id_type=pl.DeviceIdType.MESH,
        )

    def z_own(chunk):
        rows = pl.ds(pl.multiple_of(wide * capacity, 16), capacity)
        return pltpu.make_async_copy(
            z_out.at[chunk, rows, :],
            held.at[chunk, rows, :],
            z_local.at[chunk],
        )

    def scale_hidden(layer):
        hidden_copy(layer).wait()
        step_rows = 128

        @pl.loop(0, slots // step_rows)
        def _(r):
            rows = pl.ds(pl.multiple_of(r * step_rows, step_rows), step_rows)
            squares = jnp.zeros((step_rows, 128), F32)
            for k in range(features // 128):
                columns = pl.ds(k * 128, 128)
                values = hidden_buf[layer, rows, columns].astype(F32)
                gain = gain_ref[layer, columns].astype(F32)
                squares += values * values
                scaled[layer, rows, columns] = (values * gain[None, :]).astype(BF16)
            total = jnp.sum(squares.T, axis=0, keepdims=True)
            stat_out[layer, pl.ds(ADAPTER_RANK, 8), rows] = jnp.broadcast_to(total, (8, step_rows))

    def send_stats(layer):
        down_copy(layer).wait()
        down = jnp.dot(scaled[layer], down_buf[layer], preferred_element_type=F32).T
        adapter = adapter_ref[...]
        picked = jnp.zeros((ADAPTER_RANK, slots), F32)
        for a in range(ADAPTER_COUNT):
            picked += jnp.where(adapter == a, down[a * ADAPTER_RANK : (a + 1) * ADAPTER_RANK], 0.0)
        stat_out[layer, pl.ds(0, ADAPTER_RANK), :] = picked
        for d in range(1, peers):
            stat_copy(layer, d).start()

    def take_stats(layer):
        total = stat_out[layer]
        for d in range(1, peers):
            stat_copy(layer, d).wait_recv()
            total += stat_in[layer, d - 1]
        scale = lax.rsqrt(total[ADAPTER_RANK : ADAPTER_RANK + 1] / MODEL_WIDTH + EPS)
        low = ADAPTER_SCALE * scale * total[:ADAPTER_RANK]
        adapter = adapter_ref[...]
        spread = jnp.concatenate(
            [jnp.where(adapter == a, low, 0.0) for a in range(ADAPTER_COUNT)], axis=0
        )
        low_rows[layer] = spread.T.astype(BF16)
        scale_rows[layer] = jnp.broadcast_to(scale, (UNIT, slots)).T

    def make_tables():
        position = position_ref[...]
        angle = freq_ref[...] * position.astype(F32)
        cosine, sine = jnp.cos(angle), jnp.sin(angle)
        cos_tab[0] = jnp.concatenate([cosine, cosine], axis=0).T
        sin_tab[0] = jnp.concatenate([-sine, sine], axis=0).T
        cos_tab[1] = jnp.ones((slots, UNIT), F32)
        sin_tab[1] = jnp.zeros((slots, UNIT), F32)
        target = target_ref[...]
        lanes = max(width, 16)
        onehot = lax.broadcasted_iota(jnp.int32, (lanes, slots), 0) == target
        before = lax.broadcasted_iota(jnp.int32, (slots, slots), 0) <= lax.broadcasted_iota(
            jnp.int32, (slots, slots), 1
        )
        counted = jnp.dot(
            jnp.where(onehot, 1.0, 0.0).astype(BF16),
            jnp.where(before, 1.0, 0.0).astype(BF16),
            preferred_element_type=F32,
        )
        rank = jnp.sum(jnp.where(onehot, counted, 0.0), axis=0, keepdims=True).astype(jnp.int32) - 1
        place = target * capacity + rank
        place = jnp.where(position < length_ref[...], place, -1)

        @pl.loop(0, width * capacity // 128)
        def _(r):
            index = lax.broadcasted_iota(jnp.int32, (128, slots), 0) + r * 128
            pick[pl.ds(pl.multiple_of(r * 128, 128), 128), :] = jnp.where(
                index == place, 1.0, 0.0
            ).astype(BF16)

    def project(chunk):
        for copy in weight_copies(chunk):
            copy.wait()
        layer = chunk // units
        core_out[chunk] = jnp.dot(
            scaled[layer], weight_buf[chunk, :, half_cols:], preferred_element_type=F32
        ).astype(BF16)
        core_copy(chunk).start()
        own_acc[chunk] = jnp.dot(
            scaled[layer], weight_buf[chunk, :, :half_cols], preferred_element_type=F32
        )

    def pass_on(chunk):
        core_copy(chunk).wait_recv()
        for dt in range(1, tp_size):
            columns = pl.ds(dt * UNIT, UNIT)
            x_out[chunk, dt - 1] = (
                own_acc[chunk, :, columns] + core_in[chunk, :, columns].astype(F32)
            ).astype(BF16)
            x_copy(chunk, dt).start()

    def finish(chunk):
        layer, unit = chunk // units, chunk % units
        base = own_acc[chunk, :, pl.ds(0, UNIT)] + core_in[chunk, :, pl.ds(0, UNIT)].astype(F32)
        for dt in range(1, tp_size):
            x_copy(chunk, dt).wait_recv()
            base += x_in[chunk, dt - 1].astype(F32)
        fresh = scale_rows[layer] * base + jnp.dot(
            low_rows[layer],
            up_ref[layer, :, pl.ds(pl.multiple_of(unit * UNIT, UNIT), UNIT)],
            preferred_element_type=F32,
        )
        kind = unit % 2
        rotated = (
            fresh * cos_tab[kind] + pltpu.roll(fresh, HEAD_SIZE // 2, 1) * sin_tab[kind]
        ).astype(BF16)
        z_out[chunk] = jnp.dot(pick[...], rotated, preferred_element_type=F32).astype(BF16)
        for dw in range(width - 1, 0, -1):
            z_copy(chunk, dw, wide).start()
        z_own(chunk).start()

    hidden_copy(0).start()
    for copy in weight_copies(0):
        copy.start()
    down_copy(0).start()

    barrier = pltpu.get_barrier_semaphore()
    for d in range(1, peers):
        pl.semaphore_signal(barrier, inc=1, device_id=peer_id(d), device_id_type=pl.DeviceIdType.MESH)
    for dw in range(1, width):
        pl.semaphore_signal(barrier, inc=1, device_id=wide_id(dw), device_id_type=pl.DeviceIdType.MESH)

    scale_hidden(0)

    @pl.loop(1, chunks)
    def _(chunk):
        for copy in weight_copies(chunk):
            copy.start()

    for layer in range(1, layers):
        hidden_copy(layer).start()
        down_copy(layer).start()
    pl.semaphore_wait(barrier, peers - 1 + width - 1)

    @pl.loop(0, chunks + 1)
    def _(step):
        @pl.when(step == 2)
        def _():
            for layer in range(1, layers):
                scale_hidden(layer)

        @pl.when(step < chunks)
        def _():
            project(step)

        @pl.when(step == 0)
        def _():
            send_stats(0)

        @pl.when(step == 1)
        def _():
            make_tables()
            take_stats(0)

        @pl.when(step == 2)
        def _():
            for layer in range(1, layers):
                send_stats(layer)

        @pl.when(step < chunks)
        def _():
            pass_on(step)

        @pl.when(step == 3)
        def _():
            for layer in range(1, layers):
                take_stats(layer)

        @pl.when(step >= 1)
        def _():
            finish(step - 1)

    for layer in range(layers):
        for d in range(1, peers):
            stat_copy(layer, d).wait_send()

    @pl.loop(0, chunks)
    def _(chunk):
        core_copy(chunk).wait_send()
        for dt in range(1, tp_size):
            x_copy(chunk, dt).wait_send()
        for dw in range(1, width):
            z_copy(chunk, dw, wide).wait_send()
            z_copy(chunk, dw, lax.rem(wide - dw + width, width)).wait_recv()
        z_own(chunk).wait()


def store_kernel(held, out_hbm, sem):
    layers = out_hbm.shape[0]
    units = held.shape[0] // layers
    copies = [
        pltpu.make_async_copy(
            held.at[layer * units + unit],
            out_hbm.at[layer, :, pl.ds(unit * UNIT, UNIT)],
            sem.at[layer, unit],
        )
        for layer in range(layers)
        for unit in range(units)
    ]
    for copy in copies:
        copy.start()
    for copy in copies:
        copy.wait()


def shards(
    sizes_of_mesh,
    hidden,
    target_subgroup,
    token_position,
    adapter_of_row,
    request_length,
    input_norm_scale,
    key_value_weight,
    adapter_down_weight,
    adapter_up_weight,
):
    tp_size, sub_size, width = sizes_of_mesh
    layers, slots, features = hidden.shape
    block = adapter_up_weight.shape[2]
    units = block // UNIT
    chunks = layers * units
    peers = tp_size * sub_size
    capacity = 2 * slots // width
    half = HEAD_SIZE // 2
    freq = (ROPE_BASE ** (-np.arange(half) * 2.0 / HEAD_SIZE)).astype(np.float32)
    sizes = (layers, slots, features, block, tp_size, sub_size, width)
    hbm = pl.BlockSpec(memory_space=pl.ANY)
    vmem = pl.BlockSpec(memory_space=pltpu.VMEM)
    dma = pltpu.SemaphoreType.DMA
    columns = key_value_weight.shape[2]
    ranks = adapter_down_weight.shape[2]
    held = pl.pallas_call(
        functools.partial(restore_kernel, sizes),
        out_shape=pltpu.VMEM((chunks, width * capacity, UNIT), BF16),
        in_specs=[hbm, hbm, hbm] + [vmem] * 7,
        out_specs=vmem,
        scratch_shapes=[
            pltpu.VMEM((layers, slots, features), BF16),
            pltpu.VMEM((layers, slots, features), BF16),
            pltpu.VMEM((chunks, features, peers * UNIT), BF16),
            pltpu.VMEM((layers, features, ranks), BF16),
            pltpu.VMEM((chunks, slots, tp_size * UNIT), F32),
            pltpu.VMEM((chunks, slots, tp_size * UNIT), BF16),
            pltpu.VMEM((chunks, slots, tp_size * UNIT), BF16),
            pltpu.VMEM((chunks, tp_size - 1, slots, UNIT), BF16),
            pltpu.VMEM((chunks, tp_size - 1, slots, UNIT), BF16),
            pltpu.VMEM((layers, STAT_ROWS, slots), F32),
            pltpu.VMEM((layers, peers - 1, STAT_ROWS, slots), F32),
            pltpu.VMEM((layers, slots, ranks), BF16),
            pltpu.VMEM((layers, slots, UNIT), F32),
            pltpu.VMEM((2, slots, UNIT), F32),
            pltpu.VMEM((2, slots, UNIT), F32),
            pltpu.VMEM((width * capacity, slots), BF16),
            pltpu.VMEM((chunks, width * capacity, UNIT), BF16),
            dma((layers,)),
            dma((chunks, peers)),
            dma((layers,)),
            dma((chunks,)),
            dma((chunks,)),
            dma((chunks, tp_size - 1)),
            dma((chunks, tp_size - 1)),
            dma((layers, peers - 1)),
            dma((layers, peers - 1)),
            dma((chunks, width - 1)),
            dma((chunks, width - 1)),
            dma((chunks,)),
        ],
        compiler_params=pltpu.CompilerParams(
            collective_id=0, has_side_effects=True, vmem_limit_bytes=56 * 1024 * 1024
        ),
        cost_estimate=pl.CostEstimate(
            flops=2 * layers * slots * features * columns,
            bytes_accessed=2 * layers * features * columns,
            transcendentals=0,
        ),
        name="restore_rows",
    )(
        hidden,
        key_value_weight,
        adapter_down_weight,
        adapter_up_weight,
        input_norm_scale,
        target_subgroup.reshape(1, slots),
        token_position.reshape(1, slots),
        adapter_of_row.reshape(1, slots),
        request_length.reshape(1, slots),
        jnp.asarray(freq.reshape(half, 1)),
    )
    return pl.pallas_call(
        store_kernel,
        out_shape=jax.ShapeDtypeStruct((layers, width * capacity, block), BF16),
        in_specs=[vmem],
        out_specs=hbm,
        scratch_shapes=[dma((layers, units))],
        compiler_params=pltpu.CompilerParams(vmem_limit_bytes=8 * 1024 * 1024),
        name="store_rows",
    )(held)


def solution(mesh):
    sizes_of_mesh = (mesh.shape["tp"], mesh.shape["sub"], mesh.shape["wide"])
    return jax.shard_map(
        functools.partial(shards, sizes_of_mesh),
        mesh=mesh,
        in_specs=(
            P(None, ("groups", "wide"), ("tp", "sub")),
            P(("groups", "wide"), None),
            P(("groups", "wide")),
            P(("groups", "wide")),
            P(("groups", "wide")),
            P(None, ("tp", "sub")),
            P(None, ("tp", "sub"), None),
            P(None, ("tp", "sub"), None),
            P(None, None, ("tp", "sub")),
        ),
        out_specs=P(None, ("groups", "wide"), ("tp", "sub")),
        check_vma=False,
    )
```

```python
import functools

import jax
import jax.numpy as jnp
import numpy as np
from jax import lax
from jax.experimental import pallas as pl
from jax.experimental.pallas import tpu as pltpu
from jax.sharding import PartitionSpec as P

MODEL_WIDTH = 8192
HEAD_SIZE = 128
ADAPTER_COUNT = 8
ADAPTER_RANK = 16
EPS = 1e-05
ROPE_BASE = 500000.0
ADAPTER_SCALE = 2.0
UNIT = HEAD_SIZE
STAT_ROWS = 24
F32, BF16 = jnp.float32, jnp.bfloat16


def restore_kernel(
    sizes,
    hidden_hbm,
    weight_hbm,
    down_hbm,
    up_ref,
    gain_ref,
    target_ref,
    position_ref,
    adapter_ref,
    length_ref,
    freq_ref,
    held,
    hidden_buf,
    scaled,
    weight_buf,
    down_buf,
    own_acc,
    core_out,
    core_in,
    x_out,
    x_in,
    stat_out,
    stat_in,
    low_rows,
    scale_rows,
    cos_tab,
    sin_tab,
    pick,
    z_out,
    hidden_sem,
    weight_sem,
    down_sem,
    core_send,
    core_recv,
    x_send,
    x_recv,
    stat_send,
    stat_recv,
    z_send,
    z_recv,
    z_local,
):
    layers, slots, features, block, tp_size, sub_size, width = sizes
    capacity = 2 * slots // width
    units = block // UNIT
    chunks = layers * units
    peers = tp_size * sub_size
    half_cols = tp_size * UNIT

    tp = lax.axis_index("tp")
    sub = lax.axis_index("sub")
    wide = lax.axis_index("wide")

    def peer_id(d):
        dt, ds = d // sub_size, d % sub_size
        return {"tp": lax.rem(tp + dt, tp_size), "sub": lax.rem(sub + ds, sub_size)}

    def wide_id(dw):
        return {"wide": lax.rem(wide + dw, width)}

    def hidden_copy(layer):
        return pltpu.make_async_copy(hidden_hbm.at[layer], hidden_buf.at[layer], hidden_sem.at[layer])

    def down_copy(layer):
        return pltpu.make_async_copy(down_hbm.at[layer], down_buf.at[layer], down_sem.at[layer])

    def weight_copies(chunk):
        layer, unit = chunk // units, chunk % units
        copies = []
        for ds in range(sub_size):
            for dt in range(tp_size):
                t = lax.rem(tp + dt, tp_size)
                s = lax.rem(sub + ds, sub_size)
                column = pl.multiple_of((t * sub_size + s) * block + unit * UNIT, UNIT)
                place = ds * tp_size + dt
                copies.append(
                    pltpu.make_async_copy(
                        weight_hbm.at[layer, :, pl.ds(column, UNIT)],
                        weight_buf.at[chunk, :, pl.ds(place * UNIT, UNIT)],
                        weight_sem.at[chunk, place],
                    )
                )
        return copies

    def core_copy(chunk):
        return pltpu.make_async_remote_copy(
            src_ref=core_out.at[chunk],
            dst_ref=core_in.at[chunk],
            send_sem=core_send.at[chunk],
            recv_sem=core_recv.at[chunk],
            device_id={"sub": lax.rem(sub + 1, sub_size)},
            device_id_type=pl.DeviceIdType.MESH,
        )

    def x_copy(chunk, dt):
        return pltpu.make_async_remote_copy(
            src_ref=x_out.at[chunk, dt - 1],
            dst_ref=x_in.at[chunk, dt - 1],
            send_sem=x_send.at[chunk, dt - 1],
            recv_sem=x_recv.at[chunk, dt - 1],
            device_id={"tp": lax.rem(tp + dt, tp_size)},
            device_id_type=pl.DeviceIdType.MESH,
        )

    def stat_copy(layer, d):
        return pltpu.make_async_remote_copy(
            src_ref=stat_out.at[layer],
            dst_ref=stat_in.at[layer, d - 1],
            send_sem=stat_send.at[layer, d - 1],
            recv_sem=stat_recv.at[layer, d - 1],
            device_id=peer_id(d),
            device_id_type=pl.DeviceIdType.MESH,
        )

    def z_copy(chunk, dw, holder):
        goal = lax.rem(wide + dw, width)
        return pltpu.make_async_remote_copy(
            src_ref=z_out.at[chunk, pl.ds(pl.multiple_of(goal * capacity, 16), capacity), :],
            dst_ref=held.at[chunk, pl.ds(pl.multiple_of(holder * capacity, 16), capacity), :],
            send_sem=z_send.at[chunk, dw - 1],
            recv_sem=z_recv.at[chunk, dw - 1],
            device_id=wide_id(dw),
            device_id_type=pl.DeviceIdType.MESH,
        )

    def z_own(chunk):
        rows = pl.ds(pl.multiple_of(wide * capacity, 16), capacity)
        return pltpu.make_async_copy(
            z_out.at[chunk, rows, :],
            held.at[chunk, rows, :],
            z_local.at[chunk],
        )

    def scale_hidden(layer):
        hidden_copy(layer).wait()
        step_rows = 128

        @pl.loop(0, slots // step_rows)
        def _(r):
            rows = pl.ds(pl.multiple_of(r * step_rows, step_rows), step_rows)
            squares = jnp.zeros((step_rows, 128), F32)
            for k in range(features // 128):
                columns = pl.ds(k * 128, 128)
                values = hidden_buf[layer, rows, columns].astype(F32)
                gain = gain_ref[layer, columns].astype(F32)
                squares += values * values
                scaled[layer, rows, columns] = (values * gain[None, :]).astype(BF16)
            total = jnp.sum(squares.T, axis=0, keepdims=True)
            stat_out[layer, pl.ds(ADAPTER_RANK, 8), rows] = jnp.broadcast_to(total, (8, step_rows))

    def send_stats(layer):
        down_copy(layer).wait()
        down = jnp.dot(scaled[layer], down_buf[layer], preferred_element_type=F32).T
        adapter = adapter_ref[...]
        picked = jnp.zeros((ADAPTER_RANK, slots), F32)
        for a in range(ADAPTER_COUNT):
            picked += jnp.where(adapter == a, down[a * ADAPTER_RANK : (a + 1) * ADAPTER_RANK], 0.0)
        stat_out[layer, pl.ds(0, ADAPTER_RANK), :] = picked
        for d in range(1, peers):
            stat_copy(layer, d).start()

    def take_stats(layer):
        total = stat_out[layer]
        for d in range(1, peers):
            stat_copy(layer, d).wait_recv()
            total += stat_in[layer, d - 1]
        scale = lax.rsqrt(total[ADAPTER_RANK : ADAPTER_RANK + 1] / MODEL_WIDTH + EPS)
        low = ADAPTER_SCALE * scale * total[:ADAPTER_RANK]
        adapter = adapter_ref[...]
        spread = jnp.concatenate(
            [jnp.where(adapter == a, low, 0.0) for a in range(ADAPTER_COUNT)], axis=0
        )
        low_rows[layer] = spread.T.astype(BF16)
        scale_rows[layer] = jnp.broadcast_to(scale, (UNIT, slots)).T

    def make_tables():
        position = position_ref[...]
        angle = freq_ref[...] * position.astype(F32)
        cosine, sine = jnp.cos(angle), jnp.sin(angle)
        cos_tab[0] = jnp.concatenate([cosine, cosine], axis=0).T
        sin_tab[0] = jnp.concatenate([-sine, sine], axis=0).T
        cos_tab[1] = jnp.ones((slots, UNIT), F32)
        sin_tab[1] = jnp.zeros((slots, UNIT), F32)
        target = target_ref[...]
        lanes = max(width, 16)
        onehot = lax.broadcasted_iota(jnp.int32, (lanes, slots), 0) == target
        before = lax.broadcasted_iota(jnp.int32, (slots, slots), 0) <= lax.broadcasted_iota(
            jnp.int32, (slots, slots), 1
        )
        counted = jnp.dot(
            jnp.where(onehot, 1.0, 0.0).astype(BF16),
            jnp.where(before, 1.0, 0.0).astype(BF16),
            preferred_element_type=F32,
        )
        rank = jnp.sum(jnp.where(onehot, counted, 0.0), axis=0, keepdims=True).astype(jnp.int32) - 1
        place = target * capacity + rank
        place = jnp.where(position < length_ref[...], place, -1)

        @pl.loop(0, width * capacity // 128)
        def _(r):
            index = lax.broadcasted_iota(jnp.int32, (128, slots), 0) + r * 128
            pick[pl.ds(pl.multiple_of(r * 128, 128), 128), :] = jnp.where(
                index == place, 1.0, 0.0
            ).astype(BF16)

    def project(chunk):
        for copy in weight_copies(chunk):
            copy.wait()
        layer = chunk // units
        core_out[chunk] = jnp.dot(
            scaled[layer], weight_buf[chunk, :, half_cols:], preferred_element_type=F32
        ).astype(BF16)
        core_copy(chunk).start()
        own_acc[chunk] = jnp.dot(
            scaled[layer], weight_buf[chunk, :, :half_cols], preferred_element_type=F32
        )

    def pass_on(chunk):
        core_copy(chunk).wait_recv()
        for dt in range(1, tp_size):
            columns = pl.ds(dt * UNIT, UNIT)
            x_out[chunk, dt - 1] = (
                own_acc[chunk, :, columns] + core_in[chunk, :, columns].astype(F32)
            ).astype(BF16)
            x_copy(chunk, dt).start()

    def finish(chunk):
        layer, unit = chunk // units, chunk % units
        base = own_acc[chunk, :, pl.ds(0, UNIT)] + core_in[chunk, :, pl.ds(0, UNIT)].astype(F32)
        for dt in range(1, tp_size):
            x_copy(chunk, dt).wait_recv()
            base += x_in[chunk, dt - 1].astype(F32)
        fresh = scale_rows[layer] * base + jnp.dot(
            low_rows[layer],
            up_ref[layer, :, pl.ds(pl.multiple_of(unit * UNIT, UNIT), UNIT)],
            preferred_element_type=F32,
        )
        kind = unit % 2
        rotated = (
            fresh * cos_tab[kind] + pltpu.roll(fresh, HEAD_SIZE // 2, 1) * sin_tab[kind]
        ).astype(BF16)
        z_out[chunk] = jnp.dot(pick[...], rotated, preferred_element_type=F32).astype(BF16)
        low_half = 2 * wide < width
        for k in range(1, width):
            down_goal = jnp.where(width - k <= wide, width - k - 1, width - k)
            up_goal = jnp.where(k - 1 >= wide, k, k - 1)
            goal = jnp.where(low_half, down_goal, up_goal)
            z_copy(chunk, lax.rem(goal - wide + width, width), wide).start()
        z_own(chunk).start()

    hidden_copy(0).start()
    for copy in weight_copies(0):
        copy.start()
    down_copy(0).start()

    barrier = pltpu.get_barrier_semaphore()
    for d in range(1, peers):
        pl.semaphore_signal(barrier, inc=1, device_id=peer_id(d), device_id_type=pl.DeviceIdType.MESH)
    for dw in range(1, width):
        pl.semaphore_signal(barrier, inc=1, device_id=wide_id(dw), device_id_type=pl.DeviceIdType.MESH)

    scale_hidden(0)

    @pl.loop(1, chunks)
    def _(chunk):
        for copy in weight_copies(chunk):
            copy.start()

    for layer in range(1, layers):
        hidden_copy(layer).start()
        down_copy(layer).start()
    pl.semaphore_wait(barrier, peers - 1 + width - 1)

    @pl.loop(0, chunks + 1)
    def _(step):
        @pl.when(step == 2)
        def _():
            for layer in range(1, layers):
                scale_hidden(layer)

        @pl.when(step < chunks)
        def _():
            project(step)

        @pl.when(step == 0)
        def _():
            send_stats(0)

        @pl.when(step == 1)
        def _():
            make_tables()
            take_stats(0)

        @pl.when(step == 2)
        def _():
            for layer in range(1, layers):
                send_stats(layer)

        @pl.when(step < chunks)
        def _():
            pass_on(step)

        @pl.when(step == 3)
        def _():
            for layer in range(1, layers):
                take_stats(layer)

        @pl.when(step >= 1)
        def _():
            finish(step - 1)

    for layer in range(layers):
        for d in range(1, peers):
            stat_copy(layer, d).wait_send()

    @pl.loop(0, chunks)
    def _(chunk):
        core_copy(chunk).wait_send()
        for dt in range(1, tp_size):
            x_copy(chunk, dt).wait_send()
        for dw in range(1, width):
            z_copy(chunk, dw, wide).wait_send()
            z_copy(chunk, dw, lax.rem(wide - dw + width, width)).wait_recv()
        z_own(chunk).wait()


def store_kernel(held, out_hbm, sem):
    layers = out_hbm.shape[0]
    units = held.shape[0] // layers
    copies = [
        pltpu.make_async_copy(
            held.at[layer * units + unit],
            out_hbm.at[layer, :, pl.ds(unit * UNIT, UNIT)],
            sem.at[layer, unit],
        )
        for layer in range(layers)
        for unit in range(units)
    ]
    for copy in copies:
        copy.start()
    for copy in copies:
        copy.wait()


def shards(
    sizes_of_mesh,
    hidden,
    target_subgroup,
    token_position,
    adapter_of_row,
    request_length,
    input_norm_scale,
    key_value_weight,
    adapter_down_weight,
    adapter_up_weight,
):
    tp_size, sub_size, width = sizes_of_mesh
    layers, slots, features = hidden.shape
    block = adapter_up_weight.shape[2]
    units = block // UNIT
    chunks = layers * units
    peers = tp_size * sub_size
    capacity = 2 * slots // width
    half = HEAD_SIZE // 2
    freq = (ROPE_BASE ** (-np.arange(half) * 2.0 / HEAD_SIZE)).astype(np.float32)
    sizes = (layers, slots, features, block, tp_size, sub_size, width)
    hbm = pl.BlockSpec(memory_space=pl.ANY)
    vmem = pl.BlockSpec(memory_space=pltpu.VMEM)
    dma = pltpu.SemaphoreType.DMA
    columns = key_value_weight.shape[2]
    ranks = adapter_down_weight.shape[2]
    held = pl.pallas_call(
        functools.partial(restore_kernel, sizes),
        out_shape=pltpu.VMEM((chunks, width * capacity, UNIT), BF16),
        in_specs=[hbm, hbm, hbm] + [vmem] * 7,
        out_specs=vmem,
        scratch_shapes=[
            pltpu.VMEM((layers, slots, features), BF16),
            pltpu.VMEM((layers, slots, features), BF16),
            pltpu.VMEM((chunks, features, peers * UNIT), BF16),
            pltpu.VMEM((layers, features, ranks), BF16),
            pltpu.VMEM((chunks, slots, tp_size * UNIT), F32),
            pltpu.VMEM((chunks, slots, tp_size * UNIT), BF16),
            pltpu.VMEM((chunks, slots, tp_size * UNIT), BF16),
            pltpu.VMEM((chunks, tp_size - 1, slots, UNIT), BF16),
            pltpu.VMEM((chunks, tp_size - 1, slots, UNIT), BF16),
            pltpu.VMEM((layers, STAT_ROWS, slots), F32),
            pltpu.VMEM((layers, peers - 1, STAT_ROWS, slots), F32),
            pltpu.VMEM((layers, slots, ranks), BF16),
            pltpu.VMEM((layers, slots, UNIT), F32),
            pltpu.VMEM((2, slots, UNIT), F32),
            pltpu.VMEM((2, slots, UNIT), F32),
            pltpu.VMEM((width * capacity, slots), BF16),
            pltpu.VMEM((chunks, width * capacity, UNIT), BF16),
            dma((layers,)),
            dma((chunks, peers)),
            dma((layers,)),
            dma((chunks,)),
            dma((chunks,)),
            dma((chunks, tp_size - 1)),
            dma((chunks, tp_size - 1)),
            dma((layers, peers - 1)),
            dma((layers, peers - 1)),
            dma((chunks, width - 1)),
            dma((chunks, width - 1)),
            dma((chunks,)),
        ],
        compiler_params=pltpu.CompilerParams(
            collective_id=0, has_side_effects=True, vmem_limit_bytes=56 * 1024 * 1024
        ),
        cost_estimate=pl.CostEstimate(
            flops=2 * layers * slots * features * columns,
            bytes_accessed=2 * layers * features * columns,
            transcendentals=0,
        ),
        name="restore_rows",
    )(
        hidden,
        key_value_weight,
        adapter_down_weight,
        adapter_up_weight,
        input_norm_scale,
        target_subgroup.reshape(1, slots),
        token_position.reshape(1, slots),
        adapter_of_row.reshape(1, slots),
        request_length.reshape(1, slots),
        jnp.asarray(freq.reshape(half, 1)),
    )
    return pl.pallas_call(
        store_kernel,
        out_shape=jax.ShapeDtypeStruct((layers, width * capacity, block), BF16),
        in_specs=[vmem],
        out_specs=hbm,
        scratch_shapes=[dma((layers, units))],
        compiler_params=pltpu.CompilerParams(vmem_limit_bytes=8 * 1024 * 1024),
        name="store_rows",
    )(held)


def solution(mesh):
    sizes_of_mesh = (mesh.shape["tp"], mesh.shape["sub"], mesh.shape["wide"])
    return jax.shard_map(
        functools.partial(shards, sizes_of_mesh),
        mesh=mesh,
        in_specs=(
            P(None, ("groups", "wide"), ("tp", "sub")),
            P(("groups", "wide"), None),
            P(("groups", "wide")),
            P(("groups", "wide")),
            P(("groups", "wide")),
            P(None, ("tp", "sub")),
            P(None, ("tp", "sub"), None),
            P(None, ("tp", "sub"), None),
            P(None, None, ("tp", "sub")),
        ),
        out_specs=P(None, ("groups", "wide"), ("tp", "sub")),
        check_vma=False,
    )
```
